256 devices in a mesh: img: 8 (over z_lo, core), txt: 32 (over x, y, z_hi).
Axes of the slice: x: 4, y: 4, z: 8 (z_hi: 2, z_lo: 4; z = z_hi * 4 + z_lo), core: 2. Of those that a mesh axis runs over, the one named last changes fastest.
Arguments:
- images: float32 [22528, 1152], P(('img', 'txt')), may hold values from -0.18 to 0.18
- texts: float32 [22528, 1152], P(('txt', 'img')), may hold values from -0.18 to 0.18
- scale: float32 [1], replicated, may hold values from 5 to 20
- bias: float32 [1], replicated, may hold values from -3 to -1
Outputs:
- loss: float32 [1], replicated
- image_grad: float32 [22528, 1152], P(('img', 'txt'))
- text_grad: float32 [22528, 1152], P(('txt', 'img'))
The draws below stay inside these ranges and needn't reach their ends.
All inputs are finite; a program needn't handle non-finite values.
Results may differ from the reference program's by a relative error of at most 0.0006.
The reference program's roundings to bfloat16 on the way (of `coef`) count: a program that leaves them out, or rounds other values in their place, can miss the bound.
Values may be sent and summed in bfloat16 or wider, within the bound.
No kernel may reach another device: no remote copies, remote signals or barrier semaphores. Data moves between devices by JAX's collectives and lax.ppermute only.
A program may use at most 128 MiB of HBM per device.

```python
import math
import jax
import jax.numpy as jnp
from jax import lax

D = 1152
PAIRS = 22528


def steps_of(own_key, extent, pieces, smallest, high):
    def one(dim, parts):
        heights = jax.random.uniform(jax.random.fold_in(jax.random.fold_in(own_key, 6), dim), (parts,), jnp.float32, smallest / len(pieces), high / len(pieces))
        return jnp.repeat(jnp.exp(heights), extent[dim] // parts).reshape((-1,) + (1,) * (len(extent) - dim - 1))

    gain = one(*pieces[0])
    for cut in pieces[1:]:
        gain = gain * one(*cut)
    return gain


def gaussian(own_key, extent, spread, limit, cuts=(), held_as=jnp.bfloat16):
    result = spread * jax.random.normal(own_key, extent, jnp.float32)
    if cuts:
        result = result * steps_of(own_key, extent, cuts, -0.22, 0.18)
    return jnp.clip(result, -limit, limit).astype(held_as)


def setup_inputs(seed: int = 0) -> dict:
    seeds = jax.random.split(jax.random.key(seed), 5)
    images = gaussian(seeds[0], (PAIRS, D), 0.03, 0.18, ((0, 256),), jnp.float32)
    texts = gaussian(seeds[1], (PAIRS, D), 0.03, 0.18, ((0, 256),), jnp.float32)
    scale = jnp.clip(jnp.exp(jax.random.uniform(seeds[2], (1,), jnp.float32, math.log(5.0), math.log(20.0))), 5.0, 20.0)
    bias = jnp.clip(jax.random.uniform(seeds[3], (1,), jnp.float32, -3.0, -1.0), -3.0, -1.0)
    return {"images": images, "texts": texts, "scale": scale, "bias": bias}


def unit_rows(x):
    norm = jnp.sqrt(lax.optimization_barrier(jnp.sum(x * x, axis=1, keepdims=True)) + 1e-06)
    return (x / norm, norm)

def reference(images, texts, scale, bias):
    unit_img, img_norm = unit_rows(images)
    unit_txt, txt_norm = unit_rows(texts)
    img_wide = unit_img.astype(jnp.bfloat16).astype(jnp.float32)
    txt_wide = unit_txt.astype(jnp.bfloat16).astype(jnp.float32)
    factor = scale[0]
    offset = bias[0]
    block = math.gcd(PAIRS, 256)
    nblocks = PAIRS // block
    columns = jnp.arange(PAIRS, dtype=jnp.int32)

    def step(carry, index):
        txt_acc, loss_acc = carry
        start = (index * block).astype(jnp.int32)
        rows = lax.dynamic_slice_in_dim(img_wide, start, block, 0)
        logits = factor * jnp.dot(rows, txt_wide.T, precision=lax.Precision.HIGHEST, preferred_element_type=jnp.float32) + offset
        label = (start + jnp.arange(block, dtype=jnp.int32)[:, None] == columns[None, :]).astype(jnp.float32)
        loss_acc = loss_acc + jnp.sum(jax.nn.softplus(logits)) - jnp.sum(label * logits)
        coef = (jax.nn.sigmoid(logits) - label).astype(jnp.bfloat16).astype(jnp.float32)
        img_part = factor * jnp.dot(coef, txt_wide, precision=lax.Precision.HIGHEST, preferred_element_type=jnp.float32)
        txt_acc = txt_acc + factor * lax.dot_general(coef, rows, (((0,), (0,)), ((), ())), precision=lax.Precision.HIGHEST, preferred_element_type=jnp.float32)
        return ((txt_acc, loss_acc), img_part)
    init = (jnp.zeros((PAIRS, D), jnp.float32), jnp.zeros((), jnp.float32))
    (txt_grad_unit, summed), img_parts = lax.scan(step, init, jnp.arange(nblocks, dtype=jnp.int32))
    img_grad_unit = img_parts.reshape(PAIRS, D)
    image_grad = (img_grad_unit - unit_img * lax.optimization_barrier(jnp.sum(unit_img * img_grad_unit, axis=1, keepdims=True))) / img_norm
    text_grad = (txt_grad_unit - unit_txt * lax.optimization_barrier(jnp.sum(unit_txt * txt_grad_unit, axis=1, keepdims=True))) / txt_norm
    loss = (summed / (PAIRS * PAIRS)).reshape(1).astype(jnp.float32)
    return (loss, image_grad, text_grad)
```

```python
import functools
import jax
import jax.numpy as jnp
import numpy as np
from jax import lax
from jax.experimental import pallas as pl
from jax.experimental.pallas import tpu as pltpu
from jax.sharding import Mesh
from jax.sharding import PartitionSpec as P

AXES = ("zl", "c", "x", "y", "zh")
SIZES = (4, 2, 4, 4, 2)
NX, NY, NZ = 4, 4, 8
OWN = 88
BLK = 2 * OWN
SLOTS = 8
D = 1152
M = SLOTS * BLK
PAIRS = 22528
F16 = jnp.float16
F32 = jnp.float32
BF16 = jnp.bfloat16


def linear(x, y, z, c):
    return int(np.ravel_multi_index((z % 4, c, x, y, z // 4), SIZES))


def pairs_of(move, cores=(0, 1)):
    pairs = []
    for x in range(NX):
        for y in range(NY):
            for z in range(NZ):
                for c in cores:
                    to = move(x, y, z, c)
                    pairs.append((linear(x, y, z, c), linear(*to)))
    return pairs


def way(c):
    return 1 if c == 0 else -1


def along_x(sign, cores=(0, 1)):
    return pairs_of(lambda x, y, z, c: ((x + sign * way(c)) % NX, y, z, c), cores)


def along_y(sign, cores=(0, 1)):
    return pairs_of(lambda x, y, z, c: (x, (y + sign * way(c)) % NY, z, c), cores)


def along_z(sign, cores=(0, 1)):
    return pairs_of(lambda x, y, z, c: (x, y, (z + sign * way(c)) % NZ, c), cores)


def other_core():
    return pairs_of(lambda x, y, z, c: (x, y, z, 1 - c))


def send(value, pairs):
    return lax.ppermute(value, AXES, pairs)


def normalize_kernel(img_ref, txt_ref, out_ref):
    for k, ref in enumerate((img_ref, txt_ref)):
        v = ref[...]
        norm = jnp.sqrt(jnp.sum(v * v, axis=1, keepdims=True) + 1e-06)
        out_ref[k] = (v / norm).astype(BF16)


def normalize(images, texts):
    return pl.pallas_call(
        normalize_kernel,
        out_shape=jax.ShapeDtypeStruct((2, OWN, D), BF16),
        name="normalize",
    )(images, texts)


def project_kernel(sc_ref, img_ref, txt_ref, gi_ref, gt_ref, oi_ref, ot_ref):
    factor = sc_ref[0]
    for v_ref, g_ref, o_ref in ((img_ref, gi_ref, oi_ref), (txt_ref, gt_ref, ot_ref)):
        v = v_ref[...]
        norm = jnp.sqrt(jnp.sum(v * v, axis=1, keepdims=True) + 1e-06)
        unit = v / norm
        g = factor * g_ref[...]
        o_ref[...] = (g - unit * jnp.sum(unit * g, axis=1, keepdims=True)) / norm


def project(scale, images, texts, gi, gt):
    smem = pl.BlockSpec(memory_space=pltpu.SMEM)
    vmem = pl.BlockSpec(memory_space=pltpu.VMEM)
    out = jax.ShapeDtypeStruct((OWN, D), F32)
    return pl.pallas_call(
        project_kernel,
        out_shape=(out, out),
        in_specs=[smem, vmem, vmem, vmem, vmem],
        out_specs=(vmem, vmem),
        name="project",
    )(scale, images, texts, gi, gt)


ROWS = 352
COLS = 256


def score_kernel(sc_ref, bi_ref, rid_ref, cid_ref, *refs):
    imgs, txts = refs[:SLOTS], refs[SLOTS : 2 * SLOTS]
    gi_ref, gt_ref, loss_ref = refs[2 * SLOTS : 2 * SLOTS + 3]
    img, txt, coef, gi, gt, in_sem, out_sem = refs[2 * SLOTS + 3 :]
    factor = sc_ref[0]
    offset = bi_ref[0]
    loads = []
    for k in range(SLOTS):
        at = pl.ds(k * BLK, BLK)
        loads.append(pltpu.make_async_copy(txts[k], txt.at[at], in_sem.at[k]))
        loads.append(pltpu.make_async_copy(imgs[k], img.at[at], in_sem.at[SLOTS + k]))
    for load in loads:
        load.start()
    for load in loads:
        load.wait()
    total = jnp.zeros((8, M), F32)
    stores = []
    for k in range(M // ROWS):
        at = pl.ds(k * ROWS, ROWS)
        s = lax.dot_general(
            img[at, :], txt[...], (((1,), (1,)), ((), ())), preferred_element_type=F32
        )
        x = s * factor + offset
        e = jnp.exp(x)
        u = 1.0 + e
        r = 1.0 / u
        label = rid_ref[at, :] == cid_ref[...]
        coef[at, :] = jnp.where(label, -r, e * r).astype(BF16)
        term = jnp.log(u) - jnp.where(label, x, 0.0)
        total = total + jnp.sum(term.reshape(ROWS // 8, 8, M), axis=0)
        gi[at, :] = jnp.dot(coef[at, :], txt[...], preferred_element_type=F32)
        store = pltpu.make_async_copy(gi.at[at], gi_ref.at[at], out_sem.at[k])
        store.start()
        stores.append(store)
    loss_ref[...] = total
    k = M // ROWS
    for j in range(0, M, COLS):
        width = min(COLS, M - j)
        at = pl.ds(j, width)
        gt[at, :] = lax.dot_general(
            coef[:, j : j + width], img[...], (((0,), (0,)), ((), ())), preferred_element_type=F32
        )
        store = pltpu.make_async_copy(gt.at[at], gt_ref.at[at], out_sem.at[k])
        store.start()
        stores.append(store)
        k += 1
    for store in stores:
        store.wait()


def score(scale, bias, rid, cid, imgs, txts):
    smem = pl.BlockSpec(memory_space=pltpu.SMEM)
    vmem = pl.BlockSpec(memory_space=pltpu.VMEM)
    anywhere = pl.BlockSpec(memory_space=pl.ANY)
    grads = jax.ShapeDtypeStruct((M, D), F32)
    n_out = M // ROWS + -(-M // COLS)
    return pl.pallas_call(
        score_kernel,
        out_shape=(grads, grads, jax.ShapeDtypeStruct((8, M), F32)),
        in_specs=[smem, smem, vmem, vmem] + [anywhere] * (2 * SLOTS),
        out_specs=(anywhere, anywhere, vmem),
        scratch_shapes=[
            pltpu.VMEM((M, D), BF16),
            pltpu.VMEM((M, D), BF16),
            pltpu.VMEM((M, M), BF16),
            pltpu.VMEM((M, D), F32),
            pltpu.VMEM((M, D), F32),
            pltpu.SemaphoreType.DMA((2 * SLOTS,)),
            pltpu.SemaphoreType.DMA((n_out,)),
        ],
        compiler_params=pltpu.CompilerParams(vmem_limit_bytes=56 * 2**20),
        cost_estimate=pl.CostEstimate(
            flops=6 * M * M * D, bytes_accessed=12 * M * D, transcendentals=3 * M * M
        ),
        name="score",
    )(scale, bias, rid, cid, *imgs, *txts)


def on_device(images, texts, scale, bias):
    core = lax.axis_index("c")
    mx = lax.axis_index("x")
    my = lax.axis_index("y")
    zl = lax.axis_index("zl")
    zh = lax.axis_index("zh")
    mz = zh * 4 + zl
    first = core == 0

    low = normalize(images, texts)
    both = lax.all_gather(low, "c", axis=0)
    img_own = both[:, 0].reshape(BLK, D)
    txt_own = both[:, 1].reshape(BLK, D)

    fx, fy, fz = along_x(1), along_y(1), along_z(1)
    bx, by, bz = along_x(-1), along_y(-1), along_z(-1)
    swap = other_core()

    x1 = send(img_own, fx)
    y1 = send(img_own, fy)
    z1 = send(txt_own, fz)
    y2 = send(x1, fy)
    x2 = send(x1, along_x(1, (0,)))
    z2 = send(z1, fz)
    x3 = send(y2, fx)
    y3 = send(y2, fy)
    z3 = send(z2, fz)
    x4 = send(jnp.where(first, y3, x3), fx)
    y4 = send(jnp.where(first, y1, y3), fy)
    z4 = send(z3, along_z(1, (0,)))
    s2 = jnp.where(first, x2, img_own)
    t4 = jnp.where(first, z4, txt_own)
    w1, w2, w3, w4 = (send(v, swap) for v in (z1, z2, z3, t4))

    sub = jnp.arange(OWN, dtype=jnp.int32)

    def img_rows(dx, dy):
        px, py = (mx + dx) % NX, (my + dy) % NY
        ids = [((((zl * 2 + c) * 4 + px) * 4 + py) * 2 + zh) * OWN + sub for c in (0, 1)]
        return jnp.concatenate(ids)

    def txt_rows(dz):
        pz = (mz + dz) % NZ
        ids = [(((mx * 4 + my) * 2 + pz // 4) * 8 + (pz % 4) * 2 + c) * OWN + sub for c in (0, 1)]
        return jnp.concatenate(ids)

    at0 = [(-1, 0), (0, -1), (-2, 0), (-1, -1), (-2, -1), (-1, -2), (-2, -2), (0, -2)]
    at1 = [(1, 0), (0, 1), (0, 0), (1, 1), (2, 1), (1, 2), (3, 1), (1, 3)]
    rid = jnp.concatenate(
        [img_rows(jnp.where(first, a[0], b[0]), jnp.where(first, a[1], b[1])) for a, b in zip(at0, at1)]
    )
    mine = jnp.where(first, jnp.array([-1, -2, -3, -4]), jnp.array([1, 2, 3, 0]))
    theirs = jnp.where(first, jnp.array([1, 2, 3, 0]), jnp.array([-1, -2, -3, -4]))
    cid = jnp.concatenate([txt_rows(mine[k]) for k in range(4)] + [txt_rows(theirs[k]) for k in range(4)])

    gi, gt, loss_parts = score(
        scale,
        bias,
        rid[:, None],
        cid[None, :],
        (x1, y1, s2, y2, x3, y3, x4, y4),
        (z1, z2, z3, t4, w1, w2, w3, w4),
    )

    loss = jnp.sum(loss_parts).reshape(1, 1)
    loss = loss + send(loss, swap)
    for bit in (1, 2):
        loss = loss + send(loss, pairs_of(lambda x, y, z, c: (x ^ bit, y, z, c)))
    for bit in (1, 2):
        loss = loss + send(loss, pairs_of(lambda x, y, z, c: (x, y ^ bit, z, c)))
    for bit in (1, 2, 4):
        loss = loss + send(loss, pairs_of(lambda x, y, z, c: (x, y, z ^ bit, c)))
    loss = (loss / (PAIRS * PAIRS)).reshape(1)

    def low16(v):
        return v.astype(F16)

    def wide(v):
        return v.astype(F32)

    gx1, gy1, gs2, gy2, gx3, gy3, gx4, gy4 = (gi[k * BLK : (k + 1) * BLK] for k in range(SLOTS))
    gz = gt[: 4 * BLK] + wide(send(low16(gt[4 * BLK :]), swap))
    gz1, gz2, gz3, gt4 = (gz[k * BLK : (k + 1) * BLK] for k in range(4))

    r4x = wide(send(low16(gx4), bx))
    r4y = wide(send(low16(gy4), by))
    r4z = wide(send(low16(gt4), along_z(-1, (0,))))
    r3x = wide(send(low16(gx3 + jnp.where(first, 0.0, r4x)), bx))
    r3y = wide(send(low16(gy3 + jnp.where(first, r4x, r4y)), by))
    r3z = wide(send(low16(gz3 + r4z), bz))
    r2x = wide(send(low16(gs2), along_x(-1, (0,))))
    r2y = wide(send(low16(gy2 + r3x + r3y), by))
    r2z = wide(send(low16(gz2 + r3z), bz))
    r1x = wide(send(low16(gx1 + r2x + r2y), bx))
    r1y = wide(send(low16(gy1 + jnp.where(first, r4y, 0.0)), by))
    r1z = wide(send(low16(gz1 + r2z), bz))
    img_sum = r1x + r1y + jnp.where(first, 0.0, gs2)
    txt_sum = r1z + jnp.where(first, 0.0, gt4)

    own = jnp.stack([img_sum, txt_sum]).reshape(2, 2, OWN, D)
    keep = lax.dynamic_index_in_dim(own, core, 1, keepdims=False)
    give = lax.dynamic_index_in_dim(own, 1 - core, 1, keepdims=False)
    sums = keep + wide(send(low16(give), swap))
    image_grad, text_grad = project(scale, images, texts, sums[0], sums[1])
    return (loss, image_grad, text_grad)


def solution(mesh):
    fine = Mesh(np.asarray(mesh.devices).reshape(SIZES), AXES)
    img = P(("zl", "c", "x", "y", "zh"), None)
    txt = P(("x", "y", "zh", "zl", "c"), None)
    return jax.shard_map(
        on_device,
        mesh=fine,
        in_specs=(img, txt, P(), P()),
        out_specs=(P(), img, txt),
        check_vma=False,
    )
```

```python
import jax
import jax.numpy as jnp
import numpy as np
from jax import lax
from jax.experimental import pallas as pl
from jax.experimental.pallas import tpu as pltpu
from jax.sharding import Mesh
from jax.sharding import PartitionSpec as P

AXES = ("zl", "c", "x", "y", "zh")
SIZES = (4, 2, 4, 4, 2)
NX, NY, NZ = 4, 4, 8
OWN = 88
BLK = 2 * OWN
SLOTS = 8
D = 1152
M = SLOTS * BLK
PAIRS = 22528
F16 = jnp.float16
F32 = jnp.float32
BF16 = jnp.bfloat16


def linear(x, y, z, c):
    return int(np.ravel_multi_index((z % 4, c, x, y, z // 4), SIZES))


def pairs_of(move, cores=(0, 1)):
    pairs = []
    for x in range(NX):
        for y in range(NY):
            for z in range(NZ):
                for c in cores:
                    to = move(x, y, z, c)
                    pairs.append((linear(x, y, z, c), linear(*to)))
    return pairs


def way(c):
    return 1 if c == 0 else -1


def along_x(sign, cores=(0, 1)):
    return pairs_of(lambda x, y, z, c: ((x + sign * way(c)) % NX, y, z, c), cores)


def along_y(sign, cores=(0, 1)):
    return pairs_of(lambda x, y, z, c: (x, (y + sign * way(c)) % NY, z, c), cores)


def along_z(sign, cores=(0, 1)):
    return pairs_of(lambda x, y, z, c: (x, y, (z + sign * way(c)) % NZ, c), cores)


def other_core():
    return pairs_of(lambda x, y, z, c: (x, y, z, 1 - c))


def send(value, pairs):
    return lax.ppermute(value, AXES, pairs)


def normalize_kernel(img_ref, txt_ref, out_ref):
    for k, ref in enumerate((img_ref, txt_ref)):
        v = ref[...]
        norm = jnp.sqrt(jnp.sum(v * v, axis=1, keepdims=True) + 1e-06)
        out_ref[k] = (v / norm).astype(BF16)


def normalize(images, texts):
    return pl.pallas_call(
        normalize_kernel,
        out_shape=jax.ShapeDtypeStruct((2, OWN, D), BF16),
        name="normalize",
    )(images, texts)


def project_kernel(sc_ref, lean_ref, img_ref, txt_ref, keep_ref, give_ref, oi_ref, ot_ref):
    factor = sc_ref[0]
    lean = lean_ref[0] * 16.0
    for k, (v_ref, o_ref) in enumerate(((img_ref, oi_ref), (txt_ref, ot_ref))):
        v = v_ref[...]
        norm = jnp.sqrt(jnp.sum(v * v, axis=1, keepdims=True) + 1e-06)
        unit = v / norm
        g = factor * (keep_ref[k] + give_ref[k] + lean * unit.astype(BF16).astype(F32))
        o_ref[...] = (g - unit * jnp.sum(unit * g, axis=1, keepdims=True)) / norm


def project(scale, lean, images, texts, keep, give):
    smem = pl.BlockSpec(memory_space=pltpu.SMEM)
    vmem = pl.BlockSpec(memory_space=pltpu.VMEM)
    out = jax.ShapeDtypeStruct((OWN, D), F32)
    return pl.pallas_call(
        project_kernel,
        out_shape=(out, out),
        in_specs=[smem, smem, vmem, vmem, vmem, vmem],
        out_specs=(vmem, vmem),
        name="project",
    )(scale, lean, images, texts, keep, give)


IMG_AT = (
    ((-1, 0), (0, -1), (-2, 0), (-1, -1), (-2, -1), (-1, -2), (-2, -2), (0, -2)),
    ((1, 0), (0, 1), (0, 0), (1, 1), (2, 1), (1, 2), (3, 1), (1, 3)),
)
TXT_AT = ((-1, -2, -3, -4), (1, 2, 3, 0))


def block_ids():
    table = np.zeros((NX * NY * NZ * 2, 4 * SLOTS), np.int32)
    for x in range(NX):
        for y in range(NY):
            for z in range(NZ):
                for c in range(2):
                    ids = []
                    for dx, dy in IMG_AT[c]:
                        for k in range(2):
                            ids.append(linear((x + dx) % NX, (y + dy) % NY, z, k))
                    for dz in TXT_AT[c] + TXT_AT[1 - c]:
                        pz = (z + dz) % NZ
                        for k in range(2):
                            ids.append(((x * 4 + y) * 2 + pz // 4) * 8 + (pz % 4) * 2 + k)
                    table[linear(x, y, z, c)] = ids
    return table


ROWS = 352
HALF = M // 2
FIRST_I = (6, 7)
LATER_I = (5, 4, 3, 2, 0, 1)
LATER_T = (3, 2, 1, 0)


def spread(ref, start, shape, dim):
    at = lax.broadcasted_iota(jnp.int32, shape, dim)
    ids = jnp.zeros(shape, jnp.int32)
    for k in range(shape[dim] // OWN):
        shifted = (ref[0, start + k] - k) * OWN
        ids = jnp.where(at >= k * OWN, shifted, ids)
    return ids + at


def load_all(imgs, txts, img, txt, in_sem):
    loads = []
    at = 0
    for k, ref in enumerate(txts):
        n = ref.shape[0]
        loads.append(pltpu.make_async_copy(ref, txt.at[pl.ds(at, n)], in_sem.at[k]))
        at += n
    for k, ref in enumerate(imgs):
        loads.append(
            pltpu.make_async_copy(ref, img.at[pl.ds(k * BLK, BLK)], in_sem.at[len(txts) + k])
        )
    for load in loads:
        load.start()
    return loads


def score_kernel(sc_ref, bi_ref, lean_ref, ids_ref, *refs):
    imgs, txts = refs[:SLOTS], refs[SLOTS : SLOTS + 5]
    coef_ref, gx_ref, gy_ref, gw_ref, loss_ref = refs[SLOTS + 5 : SLOTS + 10]
    img, txt, coef, gi, gw, in_sem, out_sem = refs[SLOTS + 10 :]
    factor = sc_ref[0] * LOG2E
    offset = bi_ref[0] * LOG2E
    lean = lean_ref[0]
    loads = load_all(imgs, txts, img, txt, in_sem)
    cid = spread(ids_ref, 2 * SLOTS, (1, M), 1)
    for load in loads:
        load.wait()
    total = jnp.zeros((8, M), F32)
    stores = []

    def keep(src, dst):
        store = pltpu.make_async_copy(src, dst, out_sem.at[len(stores)])
        store.start()
        stores.append(store)

    for k in range(M // ROWS):
        at = pl.ds(k * ROWS, ROWS)
        s = lax.dot_general(
            img[at, :], txt[...], (((1,), (1,)), ((), ())), preferred_element_type=F32
        )
        x = s * factor + offset
        e = jnp.exp2(x)
        u = 1.0 + e
        r = 1.0 / u
        label = spread(ids_ref, 4 * k, (ROWS, 1), 0) == cid
        coef[at, :] = jnp.where(label, -r, e * r).astype(BF16)
        four = u.reshape(ROWS // 32, 4, 8, M)
        four = (four[:, 0] * four[:, 1]) * (four[:, 2] * four[:, 3])
        total = total + jnp.sum(jnp.log2(four), axis=0)
        total = total - jnp.sum(jnp.where(label, x, 0.0).reshape(ROWS // 8, 8, M), axis=0)
        keep(coef.at[at], coef_ref.at[at])
    part = total[:, :128]
    for k in range(1, M // 128):
        part = part + total[:, k * 128 : (k + 1) * 128]
    loss_ref[...] = part * LN2
    at = pl.ds(FIRST_I[0] * BLK, 2 * BLK)
    gi[...] = jnp.dot(coef[at, :], txt[...], preferred_element_type=F32) - lean * img[
        at, :
    ].astype(F32)
    keep(gi.at[pl.ds(0, BLK)], gx_ref)
    keep(gi.at[pl.ds(BLK, BLK)], gy_ref)
    for j in range(HALF, M, ROWS):
        at = pl.ds(j - HALF, ROWS)
        gw[at, :] = lax.dot_general(
            coef[:, j : j + ROWS], img[...], (((0,), (0,)), ((), ())), preferred_element_type=F32
        ) - lean * txt[pl.ds(j, ROWS), :].astype(F32)
        keep(gw.at[at], gw_ref.at[at])
    for store in stores:
        store.wait()


LOG2E = 1.4426950408889634
LN2 = 0.6931471805599453
SMEM = pl.BlockSpec(memory_space=pltpu.SMEM)
VMEM = pl.BlockSpec(memory_space=pltpu.VMEM)
ANY = pl.BlockSpec(memory_space=pl.ANY)


def score(scale, bias, lean, ids, imgs, txts):
    block = jax.ShapeDtypeStruct((BLK, D), F32)
    half = jax.ShapeDtypeStruct((HALF, D), F32)
    return pl.pallas_call(
        score_kernel,
        out_shape=(
            jax.ShapeDtypeStruct((M, M), BF16),
            block,
            block,
            half,
            jax.ShapeDtypeStruct((8, 128), F32),
        ),
        in_specs=[SMEM] * 4 + [ANY] * (SLOTS + 5),
        out_specs=(ANY, ANY, ANY, ANY, VMEM),
        scratch_shapes=[
            pltpu.VMEM((M, D), BF16),
            pltpu.VMEM((M, D), BF16),
            pltpu.VMEM((M, M), BF16),
            pltpu.VMEM((2 * BLK, D), F32),
            pltpu.VMEM((HALF, D), F32),
            pltpu.SemaphoreType.DMA((SLOTS + 5,)),
            pltpu.SemaphoreType.DMA((M // ROWS + 2 + HALF // ROWS,)),
        ],
        compiler_params=pltpu.CompilerParams(vmem_limit_bytes=48 * 2**20),
        cost_estimate=pl.CostEstimate(
            flops=4 * M * M * D, bytes_accessed=12 * M * D, transcendentals=3 * M * M
        ),
        name="score",
    )(scale, bias, lean, ids, *imgs, *txts)


def grads_kernel(lean_ref, coef_ref, *refs):
    imgs, txts = refs[:SLOTS], refs[SLOTS : SLOTS + 5]
    n = SLOTS + 5
    n_i, n_t = len(LATER_I), len(LATER_T)
    gi_refs, gt_refs = refs[n : n + n_i], refs[n + n_i : n + n_i + n_t]
    img, txt, coef, gi, gt, in_sem, out_sem = refs[n + n_i + n_t :]
    lean = lean_ref[0]
    loads = [pltpu.make_async_copy(coef_ref, coef, in_sem.at[n])]
    loads[0].start()
    loads += load_all(imgs, txts, img, txt, in_sem)
    for load in loads:
        load.wait()
    stores = []

    def keep(src, dst):
        store = pltpu.make_async_copy(src, dst, out_sem.at[len(stores)])
        store.start()
        stores.append(store)

    def img_pair(k):
        at = pl.ds(k * BLK, 2 * BLK)
        gi[at, :] = jnp.dot(coef[at, :], txt[...], preferred_element_type=F32) - lean * img[
            at, :
        ].astype(F32)
        for j in (k, k + 1):
            keep(gi.at[pl.ds(j * BLK, BLK)], gi_refs[LATER_I.index(j)])

    def txt_pair(k):
        at = pl.ds(k * BLK, 2 * BLK)
        gt[at, :] = lax.dot_general(
            coef[:, k * BLK : (k + 2) * BLK],
            img[...],
            (((0,), (0,)), ((), ())),
            preferred_element_type=F32,
        ) - lean * txt[at, :].astype(F32)
        for j in (k, k + 1):
            keep(gt.at[pl.ds(j * BLK, BLK)], gt_refs[LATER_T.index(j)])

    img_pair(4)
    txt_pair(2)
    img_pair(2)
    txt_pair(0)
    img_pair(0)
    for store in stores:
        store.wait()


def grads(lean, coef, imgs, txts):
    block = jax.ShapeDtypeStruct((BLK, D), F32)
    n_out = len(LATER_I) + len(LATER_T)
    return pl.pallas_call(
        grads_kernel,
        out_shape=(block,) * n_out,
        in_specs=[SMEM] + [ANY] * (SLOTS + 6),
        out_specs=(ANY,) * n_out,
        scratch_shapes=[
            pltpu.VMEM((M, D), BF16),
            pltpu.VMEM((M, D), BF16),
            pltpu.VMEM((M, M), BF16),
            pltpu.VMEM((6 * BLK, D), F32),
            pltpu.VMEM((HALF, D), F32),
            pltpu.SemaphoreType.DMA((SLOTS + 6,)),
            pltpu.SemaphoreType.DMA((n_out,)),
        ],
        compiler_params=pltpu.CompilerParams(vmem_limit_bytes=48 * 2**20),
        cost_estimate=pl.CostEstimate(
            flops=2 * M * M * D, bytes_accessed=12 * M * D, transcendentals=0
        ),
        name="grads",
    )(lean, coef, *imgs, *txts)


def tie(*values):
    return lax.optimization_barrier(values)


def on_device(images, texts, scale, bias):
    core = lax.axis_index("c")
    first = core == 0
    ids = lax.dynamic_slice_in_dim(jnp.asarray(block_ids()), lax.axis_index(AXES), 1, 0)

    middle = jax.nn.sigmoid(bias)
    low_end = jax.nn.sigmoid(bias - scale * np.float32(np.sqrt(3 / D)))
    high_end = jax.nn.sigmoid(bias + scale * np.float32(np.sqrt(3 / D)))
    slope = (2 / 3) * middle * (1 - middle)
    slope = slope + (1 / 6) * (low_end * (1 - low_end) + high_end * (1 - high_end))
    lean = scale * slope * np.float32(M / D)

    low = normalize(images, texts)
    both = lax.all_gather(low, "c", axis=0)
    img_own = both[:, 0].reshape(BLK, D)
    txt_own = both[:, 1].reshape(BLK, D)

    fx, fy, fz = along_x(1), along_y(1), along_z(1)
    bx, by, bz = along_x(-1), along_y(-1), along_z(-1)
    swap = other_core()

    z1 = send(txt_own, fz)
    x1 = send(img_own, fx)
    y1 = send(img_own, fy)
    z2 = send(z1, fz)
    y2 = send(x1, fy)
    x2 = send(x1, along_x(1, (0,)))
    z3 = send(z2, fz)
    x3 = send(y2, fx)
    y3 = send(y2, fy)
    z4 = send(z3, along_z(1, (0,)))
    x4 = send(jnp.where(first, y3, x3), fx)
    y4 = send(jnp.where(first, y1, y3), fy)
    s2 = jnp.where(first, x2, img_own)
    t4 = jnp.where(first, z4, txt_own)
    w = send(jnp.concatenate([z1, z2, z3, t4]), swap)

    imgs = (x1, y1, s2, y2, x3, y3, x4, y4)
    txts = (z1, z2, z3, t4, w)
    coef, gx4, gy4, gw, loss = score(scale, bias, lean, ids, imgs, txts)

    def low16(v):
        return v.astype(F16)

    def wide(v):
        return v.astype(F32)

    def flip_x(bit):
        return pairs_of(lambda x, y, z, c: (x ^ bit, y, z, c))

    def flip_y(bit):
        return pairs_of(lambda x, y, z, c: (x, y ^ bit, z, c))

    def flip_z(bit):
        return pairs_of(lambda x, y, z, c: (x, y, z ^ bit, c))

    m4x, m4y = low16(gx4), low16(gy4)
    gw = send(gw, swap)
    r4x = wide(send(m4x, bx))
    r4y = wide(send(m4y, by))
    loss = loss + send(loss, swap)
    gy3, gx3, gy2, gs2, gx1, gy1, gt4, gz3, gz2, gz1 = grads(lean, coef, imgs, txts)

    m4z = low16(gt4 + gw[3 * BLK :])
    m3x = low16(gx3 + jnp.where(first, 0.0, r4x))
    m3y = low16(gy3 + jnp.where(first, r4x, r4y))
    m4z, m3x, m3y, loss = tie(m4z, m3x, m3y, loss)
    r4z = wide(send(m4z, along_z(-1, (0,))))
    r3x = wide(send(m3x, bx))
    r3y = wide(send(m3y, by))
    loss = loss + send(loss, flip_x(1))
    r2x = wide(send(low16(gs2), along_x(-1, (0,))))

    m3z, loss = tie(low16(gz3 + gw[2 * BLK : 3 * BLK] + r4z), loss)
    r3z = wide(send(m3z, bz))
    loss = loss + send(loss, flip_x(2))
    m2y, loss = tie(low16(gy2 + r3x + r3y), loss)
    r2y = wide(send(m2y, by))
    loss = loss + send(loss, flip_y(1))
    m2z, loss = tie(low16(gz2 + gw[BLK : 2 * BLK] + r3z), loss)
    r2z = wide(send(m2z, bz))
    loss = loss + send(loss, flip_y(2))
    m1x, m1y, loss = tie(
        low16(gx1 + r2x + r2y), low16(gy1 + jnp.where(first, r4y, 0.0)), loss
    )
    r1x = wide(send(m1x, bx))
    r1y = wide(send(m1y, by))
    loss = loss + send(loss, flip_z(1))
    m1z, loss = tie(low16(gz1 + gw[:BLK] + r2z), loss)
    r1z = wide(send(m1z, bz))
    loss = loss + send(loss, flip_z(2))

    img_sum = r1x + r1y + jnp.where(first, 0.0, gs2)
    txt_sum = r1z + jnp.where(first, 0.0, gt4 + gw[3 * BLK :])
    own = jnp.stack([img_sum, txt_sum]).reshape(2, 2, OWN, D)
    keep = lax.dynamic_index_in_dim(own, core, 1, keepdims=False)
    give = lax.dynamic_index_in_dim(own, 1 - core, 1, keepdims=False)
    give, loss = tie(give, loss)
    give = send(give, swap)
    loss = loss + send(loss, flip_z(4))
    image_grad, text_grad = project(scale, lean, images, texts, keep, give)
    loss = (jnp.sum(loss) / (PAIRS * PAIRS)).reshape(1)
    return (loss, image_grad, text_grad)


def solution(mesh):
    fine = Mesh(np.asarray(mesh.devices).reshape(SIZES), AXES)
    img = P(("zl", "c", "x", "y", "zh"), None)
    txt = P(("x", "y", "zh", "zl", "c"), None)
    return jax.shard_map(
        on_device,
        mesh=fine,
        in_specs=(img, txt, P(), P()),
        out_specs=(P(), img, txt),
        check_vma=False,
    )
```

```python
import jax
import jax.numpy as jnp
import numpy as np
from jax import lax
from jax.experimental import pallas as pl
from jax.experimental.pallas import tpu as pltpu
from jax.sharding import Mesh
from jax.sharding import PartitionSpec as P

AXES = ("zl", "c", "x", "y", "zh")
SIZES = (4, 2, 4, 4, 2)
NX, NY, NZ = 4, 4, 8
OWN = 88
BLK = 2 * OWN
D = 1152
M = 16 * OWN
PAIRS = 22528
F16 = jnp.float16
F32 = jnp.float32
BF16 = jnp.bfloat16


def linear(x, y, z, c):
    return int(np.ravel_multi_index((z % 4, c, x, y, z // 4), SIZES))


def pairs_of(move):
    pairs = []
    for x in range(NX):
        for y in range(NY):
            for z in range(NZ):
                for c in (0, 1):
                    to = move(x, y, z, c)
                    pairs.append((linear(x, y, z, c), linear(*to)))
    return pairs


def along_first(step):
    return pairs_of(
        lambda x, y, z, c: ((x + step) % NX, y, z, c) if c == 0 else (x, (y + step) % NY, z, c)
    )


def along_second(step):
    return pairs_of(
        lambda x, y, z, c: (x, (y + step) % NY, z, c) if c == 0 else ((x + step) % NX, y, z, c)
    )


def along_z(step):
    return pairs_of(lambda x, y, z, c: (x, y, (z + step) % NZ, c))


def other_core():
    return pairs_of(lambda x, y, z, c: (x, y, z, 1 - c))


def send(value, pairs):
    return lax.ppermute(value, AXES, pairs)


def normalize_kernel(img_ref, txt_ref, *out_refs):
    for k, ref in enumerate((img_ref, txt_ref)):
        v = ref[...]
        norm = jnp.sqrt(jnp.sum(v * v, axis=1, keepdims=True) + 1e-06)
        out_refs[k][...] = (v / norm).astype(BF16)


def normalize(images, texts):
    return pl.pallas_call(
        normalize_kernel,
        out_shape=(jax.ShapeDtypeStruct((OWN, D), BF16),) * 2,
        name="normalize",
    )(images, texts)


def project_kernel(sc_ref, lean_ref, img_ref, txt_ref, gi_ref, gt_ref, oi_ref, ot_ref):
    factor = sc_ref[0]
    lean = lean_ref[0] * 16.0
    for v_ref, g_ref, o_ref in ((img_ref, gi_ref, oi_ref), (txt_ref, gt_ref, ot_ref)):
        v = v_ref[...]
        norm = jnp.sqrt(jnp.sum(v * v, axis=1, keepdims=True) + 1e-06)
        unit = v / norm
        g = factor * (g_ref[...] + lean * unit.astype(BF16).astype(F32))
        o_ref[...] = (g - unit * jnp.sum(unit * g, axis=1, keepdims=True)) / norm


def project(scale, lean, images, texts, gi, gt):
    smem = pl.BlockSpec(memory_space=pltpu.SMEM)
    vmem = pl.BlockSpec(memory_space=pltpu.VMEM)
    out = jax.ShapeDtypeStruct((OWN, D), F32)
    return pl.pallas_call(
        project_kernel,
        out_shape=(out, out),
        in_specs=[smem, smem, vmem, vmem, vmem, vmem],
        out_specs=(vmem, vmem),
        name="project",
    )(scale, lean, images, texts, gi, gt)


LINE = (0, -1, 1, 2)
ACROSS = (0, 1, -1, 2)
TXT_AT = (0, -1, 1, 4, 2, -3, -2, 3)
BLOCKS = 16


def block_ids():
    x, y, c = (lax.axis_index(name) for name in ("x", "y", "c"))
    zl, zh = lax.axis_index("zl"), lax.axis_index("zh")
    z = zh * 4 + zl
    imgs, txts = [], []
    for b in ACROSS:
        for a in LINE:
            px = lax.rem(x + jnp.where(c == 0, a % NX, b % NX), NX)
            py = lax.rem(y + jnp.where(c == 0, b % NY, a % NY), NY)
            imgs.append((((zl * 2 + c) * NX + px) * NY + py) * 2 + zh)
    for k in (c, 1 - c):
        for dz in TXT_AT:
            pz = lax.rem(z + dz % NZ, NZ)
            txts.append(((x * NY + y) * 2 + lax.div(pz, 4)) * 8 + lax.rem(pz, 4) * 2 + k)
    return imgs, txts


ROWS = 4 * OWN
HALF = M // 2


def spread(ids, shape, dim):
    at = lax.broadcasted_iota(jnp.int32, shape, dim)
    rows = jnp.zeros(shape, jnp.int32)
    for k, block in enumerate(ids):
        rows = jnp.where(at >= k * OWN, (block - k) * OWN, rows)
    return rows + at


def load_all(parts, whole, sem):
    loads = []
    at = 0
    for k, ref in enumerate(parts):
        n = ref.shape[0]
        loads.append(pltpu.make_async_copy(ref, whole.at[pl.ds(at, n)], sem.at[k]))
        at += n
    for load in loads:
        load.start()
    return loads


def img_grad(coef, img, txt, at, lean):
    g = jnp.dot(coef[at, :], txt[...], preferred_element_type=F32)
    return g - lean * img[at, :].astype(F32)


def txt_grad(coef, img, txt, start, size, lean):
    g = lax.dot_general(
        coef[:, start : start + size], img[...], (((0,), (0,)), ((), ())), preferred_element_type=F32
    )
    return g - lean * txt[pl.ds(start, size), :].astype(F32)


def score_kernel(sc_ref, bi_ref, lean_ref, *refs):
    imgs, txts = refs[:4], refs[4:10]
    coef_ref, gw_ref, gu_ref, gd_ref = refs[10:14]
    img, txt, coef, gt, last, img_sem, txt_sem, out_sem = refs[14:]
    factor = sc_ref[0] * LOG2E
    offset = bi_ref[0] * LOG2E
    lean = lean_ref[0]
    loads = load_all(txts, txt, txt_sem) + load_all(imgs, img, img_sem)
    img_ids, txt_ids = block_ids()
    cid = spread(txt_ids, (1, M), 1)
    for load in loads:
        load.wait()
    total = jnp.zeros((8, M), F32)
    stores = []

    def keep(src, dst):
        store = pltpu.make_async_copy(src, dst, out_sem.at[len(stores)])
        store.start()
        stores.append(store)

    for k in range(M // ROWS):
        at = pl.ds(k * ROWS, ROWS)
        s = lax.dot_general(
            img[at, :], txt[...], (((1,), (1,)), ((), ())), preferred_element_type=F32
        )
        x = s * factor + offset
        e = jnp.exp2(x)
        u = 1.0 + e
        r = 1.0 / u
        label = spread(img_ids[4 * k : 4 * k + 4], (ROWS, 1), 0) == cid
        coef[at, :] = jnp.where(label, -r, e * r).astype(BF16)
        four = u.reshape(ROWS // 32, 4, 8, M)
        four = (four[:, 0] * four[:, 1]) * (four[:, 2] * four[:, 3])
        total = total + jnp.sum(jnp.log2(four), axis=0)
        total = total - jnp.sum(jnp.where(label, x, 0.0).reshape(ROWS // 8, 8, M), axis=0)
        keep(coef.at[at], coef_ref.at[at])
    part = total[:, :128]
    for k in range(1, M // 128):
        part = part + total[:, k * 128 : (k + 1) * 128]
    last[...] = jnp.zeros((8, D), F32)
    last[:, :128] = part * LN2
    keep(last, gw_ref.at[pl.ds(HALF, 8)])
    at = pl.ds(0, HALF)
    gt[at, :] = txt_grad(coef, img, txt, HALF, HALF, lean)
    keep(gt.at[at], gw_ref.at[at])
    at = pl.ds(HALF, ROWS)
    gt[at, :] = txt_grad(coef, img, txt, ROWS, ROWS, lean)
    keep(gt.at[pl.ds(HALF, BLK)], gu_ref)
    keep(gt.at[pl.ds(HALF + BLK, BLK)], gd_ref)
    for store in stores:
        store.wait()


LOG2E = 1.4426950408889634
LN2 = 0.6931471805599453
SMEM = pl.BlockSpec(memory_space=pltpu.SMEM)
VMEM = pl.BlockSpec(memory_space=pltpu.VMEM)
ANY = pl.BlockSpec(memory_space=pl.ANY)


def f32(rows):
    return jax.ShapeDtypeStruct((rows, D), F32)


def score(scale, bias, lean, imgs, txts):
    return pl.pallas_call(
        score_kernel,
        out_shape=(
            jax.ShapeDtypeStruct((M, M), BF16),
            f32(HALF + 8),
            f32(BLK),
            f32(BLK),
        ),
        in_specs=[SMEM] * 3 + [ANY] * 10,
        out_specs=(ANY,) * 4,
        scratch_shapes=[
            pltpu.VMEM((M, D), BF16),
            pltpu.VMEM((M, D), BF16),
            pltpu.VMEM((M, M), BF16),
            pltpu.VMEM((3 * ROWS, D), F32),
            pltpu.VMEM((8, D), F32),
            pltpu.SemaphoreType.DMA((4,)),
            pltpu.SemaphoreType.DMA((6,)),
            pltpu.SemaphoreType.DMA((M // ROWS + 4,)),
        ],
        compiler_params=pltpu.CompilerParams(vmem_limit_bytes=48 * 2**20),
        cost_estimate=pl.CostEstimate(
            flops=4 * M * M * D, bytes_accessed=12 * M * D, transcendentals=3 * M * M
        ),
        name="score",
    )(scale, bias, lean, *imgs, *txts)


def across_kernel(lean_ref, coef_ref, *refs):
    imgs, txts, out_refs = refs[:3], refs[3:9], refs[9:12]
    img, txt, coef, gi, img_sem, txt_sem, coef_sem, out_sem = refs[12:]
    lean = lean_ref[0]
    loads = [pltpu.make_async_copy(coef_ref.at[pl.ds(ROWS, 3 * ROWS)], coef, coef_sem)]
    loads[0].start()
    loads += load_all(txts, txt, txt_sem) + load_all(imgs, img, img_sem)
    for load in loads:
        load.wait()
    stores = []
    for k, dst in enumerate(out_refs):
        at = pl.ds(k * ROWS, ROWS)
        gi[at, :] = img_grad(coef, img, txt, at, lean)
        store = pltpu.make_async_copy(gi.at[at], dst, out_sem.at[k])
        store.start()
        stores.append(store)
    for store in stores:
        store.wait()


def across(lean, coef, imgs, txts):
    return pl.pallas_call(
        across_kernel,
        out_shape=(f32(ROWS),) * 3,
        in_specs=[SMEM] + [ANY] * 10,
        out_specs=(ANY,) * 3,
        scratch_shapes=[
            pltpu.VMEM((3 * ROWS, D), BF16),
            pltpu.VMEM((M, D), BF16),
            pltpu.VMEM((3 * ROWS, M), BF16),
            pltpu.VMEM((3 * ROWS, D), F32),
            pltpu.SemaphoreType.DMA((3,)),
            pltpu.SemaphoreType.DMA((6,)),
            pltpu.SemaphoreType.DMA,
            pltpu.SemaphoreType.DMA((3,)),
        ],
        compiler_params=pltpu.CompilerParams(vmem_limit_bytes=48 * 2**20),
        cost_estimate=pl.CostEstimate(
            flops=2 * 3 * ROWS * M * D, bytes_accessed=8 * M * D, transcendentals=0
        ),
        name="across",
    )(lean, coef, *imgs, *txts)


def near_kernel(lean_ref, coef_ref, *refs):
    imgs, txts, gl_ref, gf_ref = refs[:4], refs[4:10], refs[10], refs[11]
    img, txt, coef, gi, gt, img_sem, txt_sem, coef_sem, out_sem = refs[12:]
    lean = lean_ref[0]
    loads = [pltpu.make_async_copy(coef_ref, coef, coef_sem)]
    loads[0].start()
    loads += load_all(imgs, img, img_sem) + load_all(txts, txt, txt_sem)
    for load in loads:
        load.wait()
    gt[...] = txt_grad(coef, img, txt, 0, ROWS, lean)
    first = pltpu.make_async_copy(gt, gf_ref, out_sem.at[0])
    first.start()
    gi[...] = img_grad(coef, img, txt, pl.ds(0, ROWS), lean)
    second = pltpu.make_async_copy(gi, gl_ref, out_sem.at[1])
    second.start()
    first.wait()
    second.wait()


def nearby(lean, coef, imgs, txts):
    return pl.pallas_call(
        near_kernel,
        out_shape=(f32(ROWS),) * 2,
        in_specs=[SMEM] + [ANY] * 11,
        out_specs=(ANY,) * 2,
        scratch_shapes=[
            pltpu.VMEM((M, D), BF16),
            pltpu.VMEM((M, D), BF16),
            pltpu.VMEM((M, M), BF16),
            pltpu.VMEM((ROWS, D), F32),
            pltpu.VMEM((ROWS, D), F32),
            pltpu.SemaphoreType.DMA((4,)),
            pltpu.SemaphoreType.DMA((6,)),
            pltpu.SemaphoreType.DMA,
            pltpu.SemaphoreType.DMA((2,)),
        ],
        compiler_params=pltpu.CompilerParams(vmem_limit_bytes=48 * 2**20),
        cost_estimate=pl.CostEstimate(
            flops=M * M * D, bytes_accessed=12 * M * D, transcendentals=0
        ),
        name="nearby",
    )(lean, coef, *imgs, *txts)


def tie(*values):
    return lax.optimization_barrier(values)


def on_device(images, texts, scale, bias):
    middle = jax.nn.sigmoid(bias)
    low_end = jax.nn.sigmoid(bias - scale * np.float32(np.sqrt(3 / D)))
    high_end = jax.nn.sigmoid(bias + scale * np.float32(np.sqrt(3 / D)))
    slope = (2 / 3) * middle * (1 - middle)
    slope = slope + (1 / 6) * (low_end * (1 - low_end) + high_end * (1 - high_end))
    lean = scale * slope * np.float32(M / D)

    img, txt = normalize(images, texts)
    swap = other_core()

    t4 = send(txt, along_z(4))
    i_n, i_p = send(img, along_first(1)), send(img, along_first(-1))
    i2 = send(img, along_first(-2))
    tp = send(txt, along_z(-1))
    txt_late, i_n = tie(txt, i_n)
    tn = send(txt_late, along_z(1))
    line = jnp.concatenate([img, i_n, i_p, i2])
    qp, qn = send(line, along_second(-1)), send(line, along_second(1))
    line_late, tp = tie(line, tp)
    q2 = send(line_late, along_second(-2))
    up = send(jnp.concatenate([tp, t4]), along_z(-1))
    down = send(jnp.concatenate([tn, t4]), along_z(1))
    fan = jnp.concatenate([txt, tn, tp, t4])
    fan, qp = tie(fan, qp)
    fan_w = send(fan, swap)
    up_w, down_w = send(up, swap), send(down, swap)

    imgs = (line, qp, qn, q2)
    txts = (fan, up, down, fan_w, up_w, down_w)
    coef, gw, gup, gdown = score(scale, bias, lean, imgs, txts)

    def low16(v):
        return v.astype(F16)

    def wide(v):
        return v.astype(F32)

    def limbs(value):
        high = jnp.floor(value / 2048.0)
        rest = value - 2048.0 * high
        middle = jnp.floor(rest)
        last = jnp.floor((rest - middle) * 2048.0)
        return jnp.concatenate([high, middle, last], axis=1)

    def value_of(parts):
        return parts[:, :128] * 2048.0 + (parts[:, 128:256] + parts[:, 256:] / 2048.0)

    def tagged(rows, parts):
        return jnp.concatenate([low16(rows), low16(jnp.pad(parts, ((0, 0), (0, D - 384))))])

    def tag_of(message):
        return wide(message[-8:, :384])

    loss = gw[HALF:, :128]
    gw = send(gw, swap)
    loss = loss + gw[HALF:, :128]
    gp, gn, g2 = across(lean, coef, imgs[1:], txts)
    m_up = low16(gup + gw[ROWS : ROWS + BLK])
    m_down = low16(gdown + gw[ROWS + BLK : HALF])
    from_n = send(m_up, along_z(1))
    from_p = send(m_down, along_z(-1))
    tag = limbs(loss)
    r2 = send(tagged(g2, tag), along_second(2))
    rp = send(tagged(gp, tag), along_second(1))
    rn = send(tagged(gn, tag), along_second(-1))
    late, m_up, m_down, gn = tie(coef, m_up, m_down, gn)
    gline, gfan = nearby(lean, late, imgs, txts)
    gfan = gfan + gw[:ROWS]
    fan_4 = gfan[3 * OWN :] + wide(from_n[OWN:]) + wide(from_p[OWN:])
    fan_p = gfan[2 * OWN : 3 * OWN] + wide(from_n[:OWN])
    fan_n = gfan[OWN : 2 * OWN] + wide(from_p[:OWN])
    e4 = send(low16(fan_4), along_z(4))
    ep = send(low16(fan_p), along_z(1))
    en = send(low16(fan_n), along_z(-1))
    gline = gline + (wide(rp[:ROWS]) + wide(rn[:ROWS]) + wide(r2[:ROWS]))
    tag = limbs(value_of(tag + tag_of(rp) + tag_of(rn) + tag_of(r2)))
    d2 = send(tagged(gline[3 * OWN :], tag), along_first(2))
    dp = send(tagged(gline[2 * OWN : 3 * OWN], tag), along_first(1))
    dn = send(tagged(gline[OWN : 2 * OWN], tag), along_first(-1))
    loss = value_of(tag + tag_of(dp) + tag_of(dn) + tag_of(d2))
    loss = lax.all_to_all(jnp.tile(loss, (NZ, 1)), ("zh", "zl"), 0, 0, tiled=True)
    txt_sum = gfan[:OWN] + (wide(e4) + wide(ep) + wide(en))
    img_sum = gline[:OWN] + (wide(d2[:OWN]) + wide(dp[:OWN]) + wide(dn[:OWN]))
    image_grad, text_grad = project(scale, lean, images, texts, img_sum, txt_sum)
    loss = (jnp.sum(loss) / (PAIRS * PAIRS)).reshape(1)
    return (loss, image_grad, text_grad)


def solution(mesh):
    fine = Mesh(np.asarray(mesh.devices).reshape(SIZES), AXES)
    img = P(("zl", "c", "x", "y", "zh"), None)
    txt = P(("x", "y", "zh", "zl", "c"), None)
    return jax.shard_map(
        on_device,
        mesh=fine,
        in_specs=(img, txt, P(), P()),
        out_specs=(P(), img, txt),
        check_vma=False,
    )
```

```python
import jax
import jax.numpy as jnp
import numpy as np
from jax import lax
from jax.experimental import pallas as pl
from jax.experimental.pallas import tpu as pltpu
from jax.sharding import Mesh
from jax.sharding import PartitionSpec as P

AXES = ("zl", "c", "x", "y", "zh")
SIZES = (4, 2, 4, 4, 2)
NX, NY, NZ = 4, 4, 8
OWN = 88
BLK = 2 * OWN
D = 1152
M = 16 * OWN
PAIRS = 22528
F16 = jnp.float16
F32 = jnp.float32
BF16 = jnp.bfloat16


def linear(x, y, z, c):
    return int(np.ravel_multi_index((z % 4, c, x, y, z // 4), SIZES))


def pairs_of(move):
    pairs = []
    for x in range(NX):
        for y in range(NY):
            for z in range(NZ):
                for c in (0, 1):
                    to = move(x, y, z, c)
                    pairs.append((linear(x, y, z, c), linear(*to)))
    return pairs


def along_first(step):
    return pairs_of(
        lambda x, y, z, c: ((x + step) % NX, y, z, c) if c == 0 else (x, (y + step) % NY, z, c)
    )


def along_second(step):
    return pairs_of(
        lambda x, y, z, c: (x, (y + step) % NY, z, c) if c == 0 else ((x + step) % NX, y, z, c)
    )


def along_z(step):
    return pairs_of(lambda x, y, z, c: (x, y, (z + step) % NZ, c))


def other_core():
    return pairs_of(lambda x, y, z, c: (x, y, z, 1 - c))


def send(value, pairs):
    return lax.ppermute(value, AXES, pairs)


def normalize_kernel(img_ref, txt_ref, *out_refs):
    for k, ref in enumerate((img_ref, txt_ref)):
        v = ref[...]
        norm = jnp.sqrt(jnp.sum(v * v, axis=1, keepdims=True) + 1e-06)
        out_refs[k][...] = (v / norm).astype(BF16)


def normalize(images, texts):
    return pl.pallas_call(
        normalize_kernel,
        out_shape=(jax.ShapeDtypeStruct((OWN, D), BF16),) * 2,
        name="normalize",
    )(images, texts)


def project_kernel(sc_ref, lean_ref, img_ref, txt_ref, gi_ref, gt_ref, oi_ref, ot_ref):
    factor = sc_ref[0]
    lean = lean_ref[0] * 16.0
    for v_ref, g_ref, o_ref in ((img_ref, gi_ref, oi_ref), (txt_ref, gt_ref, ot_ref)):
        v = v_ref[...]
        norm = jnp.sqrt(jnp.sum(v * v, axis=1, keepdims=True) + 1e-06)
        unit = v / norm
        g = factor * (g_ref[...] + lean * unit.astype(BF16).astype(F32))
        o_ref[...] = (g - unit * jnp.sum(unit * g, axis=1, keepdims=True)) / norm


def project(scale, lean, images, texts, gi, gt):
    smem = pl.BlockSpec(memory_space=pltpu.SMEM)
    vmem = pl.BlockSpec(memory_space=pltpu.VMEM)
    out = jax.ShapeDtypeStruct((OWN, D), F32)
    return pl.pallas_call(
        project_kernel,
        out_shape=(out, out),
        in_specs=[smem, smem, vmem, vmem, vmem, vmem],
        out_specs=(vmem, vmem),
        name="project",
    )(scale, lean, images, texts, gi, gt)


LINE = (0, -1, 1, 2)
ACROSS = (0, 1, -1, 2)
TXT_AT = (0, -1, 1, 4, 2, -3, -2, 3)
BLOCKS = 16


def block_ids():
    x, y, c = (lax.axis_index(name) for name in ("x", "y", "c"))
    zl, zh = lax.axis_index("zl"), lax.axis_index("zh")
    z = zh * 4 + zl
    imgs, txts = [], []
    for b in ACROSS:
        for a in LINE:
            px = lax.rem(x + jnp.where(c == 0, a % NX, b % NX), NX)
            py = lax.rem(y + jnp.where(c == 0, b % NY, a % NY), NY)
            imgs.append((((zl * 2 + c) * NX + px) * NY + py) * 2 + zh)
    for k in (c, 1 - c):
        for dz in TXT_AT:
            pz = lax.rem(z + dz % NZ, NZ)
            txts.append(((x * NY + y) * 2 + lax.div(pz, 4)) * 8 + lax.rem(pz, 4) * 2 + k)
    return imgs, txts


ROWS = 4 * OWN
HALF = M // 2


def spread(ids, shape, dim):
    at = lax.broadcasted_iota(jnp.int32, shape, dim)
    rows = jnp.zeros(shape, jnp.int32)
    for k, block in enumerate(ids):
        rows = jnp.where(at >= k * OWN, (block - k) * OWN, rows)
    return rows + at


def load_all(parts, whole, sem):
    loads = []
    at = 0
    for k, ref in enumerate(parts):
        n = ref.shape[0]
        loads.append(pltpu.make_async_copy(ref, whole.at[pl.ds(at, n)], sem.at[k]))
        at += n
    for load in loads:
        load.start()
    return loads


def img_grad(coef, img, txt, at, lean):
    g = jnp.dot(coef[at, :], txt[...], preferred_element_type=F32)
    return g - lean * img[at, :].astype(F32)


def txt_grad(coef, img, txt, start, size, lean):
    g = lax.dot_general(
        coef[:, start : start + size], img[...], (((0,), (0,)), ((), ())), preferred_element_type=F32
    )
    return g - lean * txt[pl.ds(start, size), :].astype(F32)


def score_kernel(sc_ref, bi_ref, lean_ref, *refs):
    imgs, txts = refs[:4], refs[4:10]
    coef_ref, gw_ref, gu_ref, gd_ref = refs[10:14]
    img, txt, coef, gt, last, img_sem, txt_sem, out_sem = refs[14:]
    factor = sc_ref[0] * LOG2E
    offset = bi_ref[0] * LOG2E
    lean = lean_ref[0]
    loads = load_all(txts, txt, txt_sem) + load_all(imgs, img, img_sem)
    img_ids, txt_ids = block_ids()
    cid = spread(txt_ids, (1, M), 1)
    for load in loads:
        load.wait()
    total = jnp.zeros((8, M), F32)
    stores = []

    def keep(src, dst):
        store = pltpu.make_async_copy(src, dst, out_sem.at[len(stores)])
        store.start()
        stores.append(store)

    for k in range(M // ROWS):
        at = pl.ds(k * ROWS, ROWS)
        s = lax.dot_general(
            img[at, :], txt[...], (((1,), (1,)), ((), ())), preferred_element_type=F32
        )
        x = s * factor + offset
        e = jnp.exp2(x)
        u = 1.0 + e
        r = 1.0 / u
        label = spread(img_ids[4 * k : 4 * k + 4], (ROWS, 1), 0) == cid
        coef[at, :] = jnp.where(label, -r, e * r).astype(BF16)
        four = u.reshape(ROWS // 32, 4, 8, M)
        four = (four[:, 0] * four[:, 1]) * (four[:, 2] * four[:, 3])
        total = total + jnp.sum(jnp.log2(four), axis=0)
        total = total - jnp.sum(jnp.where(label, x, 0.0).reshape(ROWS // 8, 8, M), axis=0)
        keep(coef.at[at], coef_ref.at[at])
    part = total[:, :128]
    for k in range(1, M // 128):
        part = part + total[:, k * 128 : (k + 1) * 128]
    last[...] = jnp.zeros((8, D), F32)
    last[:, :128] = part * LN2
    keep(last, gw_ref.at[pl.ds(HALF, 8)])
    at = pl.ds(0, HALF)
    gt[at, :] = txt_grad(coef, img, txt, HALF, HALF, lean)
    keep(gt.at[at], gw_ref.at[at])
    at = pl.ds(HALF, ROWS)
    gt[at, :] = txt_grad(coef, img, txt, ROWS, ROWS, lean)
    keep(gt.at[pl.ds(HALF, BLK)], gu_ref)
    keep(gt.at[pl.ds(HALF + BLK, BLK)], gd_ref)
    for store in stores:
        store.wait()


LOG2E = 1.4426950408889634
LN2 = 0.6931471805599453
SMEM = pl.BlockSpec(memory_space=pltpu.SMEM)
VMEM = pl.BlockSpec(memory_space=pltpu.VMEM)
ANY = pl.BlockSpec(memory_space=pl.ANY)


def f32(rows):
    return jax.ShapeDtypeStruct((rows, D), F32)


def score(scale, bias, lean, imgs, txts):
    return pl.pallas_call(
        score_kernel,
        out_shape=(
            jax.ShapeDtypeStruct((M, M), BF16),
            f32(HALF + 8),
            f32(BLK),
            f32(BLK),
        ),
        in_specs=[SMEM] * 3 + [ANY] * 10,
        out_specs=(ANY,) * 4,
        scratch_shapes=[
            pltpu.VMEM((M, D), BF16),
            pltpu.VMEM((M, D), BF16),
            pltpu.VMEM((M, M), BF16),
            pltpu.VMEM((3 * ROWS, D), F32),
            pltpu.VMEM((8, D), F32),
            pltpu.SemaphoreType.DMA((4,)),
            pltpu.SemaphoreType.DMA((6,)),
            pltpu.SemaphoreType.DMA((M // ROWS + 4,)),
        ],
        compiler_params=pltpu.CompilerParams(vmem_limit_bytes=42 * 2**20),
        cost_estimate=pl.CostEstimate(
            flops=4 * M * M * D, bytes_accessed=12 * M * D, transcendentals=3 * M * M
        ),
        name="score",
    )(scale, bias, lean, *imgs, *txts)


def across_kernel(lean_ref, coef_ref, *refs):
    imgs, txts, out_refs = refs[:3], refs[3:9], refs[9:12]
    img, txt, coef, gi, img_sem, txt_sem, coef_sem, out_sem = refs[12:]
    lean = lean_ref[0]
    loads = [pltpu.make_async_copy(coef_ref.at[pl.ds(ROWS, 3 * ROWS)], coef, coef_sem)]
    loads[0].start()
    loads += load_all(txts, txt, txt_sem) + load_all(imgs, img, img_sem)
    for load in loads:
        load.wait()
    stores = []
    for k, dst in enumerate(out_refs):
        at = pl.ds(k * ROWS, ROWS)
        gi[at, :] = img_grad(coef, img, txt, at, lean)
        store = pltpu.make_async_copy(gi.at[at], dst, out_sem.at[k])
        store.start()
        stores.append(store)
    for store in stores:
        store.wait()


def across(lean, coef, imgs, txts):
    return pl.pallas_call(
        across_kernel,
        out_shape=(f32(ROWS),) * 3,
        in_specs=[SMEM] + [ANY] * 10,
        out_specs=(ANY,) * 3,
        scratch_shapes=[
            pltpu.VMEM((3 * ROWS, D), BF16),
            pltpu.VMEM((M, D), BF16),
            pltpu.VMEM((3 * ROWS, M), BF16),
            pltpu.VMEM((3 * ROWS, D), F32),
            pltpu.SemaphoreType.DMA((3,)),
            pltpu.SemaphoreType.DMA((6,)),
            pltpu.SemaphoreType.DMA,
            pltpu.SemaphoreType.DMA((3,)),
        ],
        compiler_params=pltpu.CompilerParams(vmem_limit_bytes=24 * 2**20),
        cost_estimate=pl.CostEstimate(
            flops=2 * 3 * ROWS * M * D, bytes_accessed=8 * M * D, transcendentals=0
        ),
        name="across",
    )(lean, coef, *imgs, *txts)


def near_kernel(lean_ref, coef_ref, *refs):
    imgs, txts, gl_ref, gf_ref = refs[:4], refs[4:10], refs[10], refs[11]
    img, txt, coef, gi, gt, img_sem, txt_sem, coef_sem, out_sem = refs[12:]
    lean = lean_ref[0]
    loads = [pltpu.make_async_copy(coef_ref, coef, coef_sem)]
    loads[0].start()
    loads += load_all(imgs, img, img_sem) + load_all(txts, txt, txt_sem)
    for load in loads:
        load.wait()
    gt[...] = txt_grad(coef, img, txt, 0, ROWS, lean)
    first = pltpu.make_async_copy(gt, gf_ref, out_sem.at[0])
    first.start()
    gi[...] = img_grad(coef, img, txt, pl.ds(0, ROWS), lean)
    second = pltpu.make_async_copy(gi, gl_ref, out_sem.at[1])
    second.start()
    first.wait()
    second.wait()


def nearby(lean, coef, imgs, txts):
    return pl.pallas_call(
        near_kernel,
        out_shape=(f32(ROWS),) * 2,
        in_specs=[SMEM] + [ANY] * 11,
        out_specs=(ANY,) * 2,
        scratch_shapes=[
            pltpu.VMEM((M, D), BF16),
            pltpu.VMEM((M, D), BF16),
            pltpu.VMEM((M, M), BF16),
            pltpu.VMEM((ROWS, D), F32),
            pltpu.VMEM((ROWS, D), F32),
            pltpu.SemaphoreType.DMA((4,)),
            pltpu.SemaphoreType.DMA((6,)),
            pltpu.SemaphoreType.DMA,
            pltpu.SemaphoreType.DMA((2,)),
        ],
        compiler_params=pltpu.CompilerParams(vmem_limit_bytes=24 * 2**20),
        cost_estimate=pl.CostEstimate(
            flops=M * M * D, bytes_accessed=12 * M * D, transcendentals=0
        ),
        name="nearby",
    )(lean, coef, *imgs, *txts)


def tie(*values):
    return lax.optimization_barrier(values)


def on_device(images, texts, scale, bias):
    middle = jax.nn.sigmoid(bias)
    low_end = jax.nn.sigmoid(bias - scale * np.float32(np.sqrt(3 / D)))
    high_end = jax.nn.sigmoid(bias + scale * np.float32(np.sqrt(3 / D)))
    slope = (2 / 3) * middle * (1 - middle)
    slope = slope + (1 / 6) * (low_end * (1 - low_end) + high_end * (1 - high_end))
    lean = scale * slope * np.float32(M / D)

    img, txt = normalize(images, texts)
    swap = other_core()

    t4 = send(txt, along_z(4))
    i_n, i_p = send(img, along_first(1)), send(img, along_first(-1))
    i2 = send(img, along_first(-2))
    tp = send(txt, along_z(-1))
    txt_late, i_n = tie(txt, i_n)
    tn = send(txt_late, along_z(1))
    line = jnp.concatenate([img, i_n, i_p, i2])
    qp, qn = send(line, along_second(-1)), send(line, along_second(1))
    line_late, tp = tie(line, tp)
    q2 = send(line_late, along_second(-2))
    up = send(jnp.concatenate([tp, t4]), along_z(-1))
    down = send(jnp.concatenate([tn, t4]), along_z(1))
    fan = jnp.concatenate([txt, tn, tp, t4])
    fan, qp = tie(fan, qp)
    fan_w = send(fan, swap)
    up_w, down_w = send(up, swap), send(down, swap)

    imgs = (line, qp, qn, q2)
    txts = (fan, up, down, fan_w, up_w, down_w)
    coef, gw, gup, gdown = score(scale, bias, lean, imgs, txts)

    def low16(v):
        return v.astype(F16)

    def wide(v):
        return v.astype(F32)

    def limbs(value):
        high = jnp.floor(value / 2048.0)
        rest = value - 2048.0 * high
        middle = jnp.floor(rest)
        last = jnp.floor((rest - middle) * 2048.0)
        return jnp.concatenate([high, middle, last], axis=1)

    def value_of(parts):
        return parts[:, :128] * 2048.0 + (parts[:, 128:256] + parts[:, 256:] / 2048.0)

    def tagged(rows, parts):
        return jnp.concatenate([low16(rows), low16(jnp.pad(parts, ((0, 0), (0, D - 384))))])

    def tag_of(message):
        return wide(message[-8:, :384])

    loss = gw[HALF:, :128]
    gw = send(gw, swap)
    loss = loss + gw[HALF:, :128]
    gp, gn, g2 = across(lean, coef, imgs[1:], txts)
    m_up = low16(gup + gw[ROWS : ROWS + BLK])
    m_down = low16(gdown + gw[ROWS + BLK : HALF])
    from_n = send(m_up, along_z(1))
    from_p = send(m_down, along_z(-1))
    tag = limbs(loss)
    r2 = send(tagged(g2, tag), along_second(2))
    rp = send(tagged(gp, tag), along_second(1))
    rn = send(tagged(gn, tag), along_second(-1))
    late, m_up, m_down, gn = tie(coef, m_up, m_down, gn)
    gline, gfan = nearby(lean, late, imgs, txts)
    gfan = gfan + gw[:ROWS]
    fan_4 = gfan[3 * OWN :] + wide(from_n[OWN:]) + wide(from_p[OWN:])
    fan_p = gfan[2 * OWN : 3 * OWN] + wide(from_n[:OWN])
    fan_n = gfan[OWN : 2 * OWN] + wide(from_p[:OWN])
    e4 = send(low16(fan_4), along_z(4))
    ep = send(low16(fan_p), along_z(1))
    en = send(low16(fan_n), along_z(-1))
    gline = gline + (wide(rp[:ROWS]) + wide(rn[:ROWS]) + wide(r2[:ROWS]))
    tag = limbs(value_of(tag + tag_of(rp) + tag_of(rn) + tag_of(r2)))
    d2 = send(tagged(gline[3 * OWN :], tag), along_first(2))
    dp = send(tagged(gline[2 * OWN : 3 * OWN], tag), along_first(1))
    dn = send(tagged(gline[OWN : 2 * OWN], tag), along_first(-1))
    loss = value_of(tag + tag_of(dp) + tag_of(dn) + tag_of(d2))
    loss = lax.all_to_all(jnp.tile(loss, (NZ, 1)), ("zh", "zl"), 0, 0, tiled=True)
    txt_sum = gfan[:OWN] + (wide(e4) + wide(ep) + wide(en))
    img_sum = gline[:OWN] + (wide(d2[:OWN]) + wide(dp[:OWN]) + wide(dn[:OWN]))
    image_grad, text_grad = project(scale, lean, images, texts, img_sum, txt_sum)
    loss = (jnp.sum(loss) / (PAIRS * PAIRS)).reshape(1)
    return (loss, image_grad, text_grad)


def solution(mesh):
    fine = Mesh(np.asarray(mesh.devices).reshape(SIZES), AXES)
    img = P(("zl", "c", "x", "y", "zh"), None)
    txt = P(("x", "y", "zh", "zl", "c"), None)
    return jax.shard_map(
        on_device,
        mesh=fine,
        in_specs=(img, txt, P(), P()),
        out_specs=(P(), img, txt),
        check_vma=False,
    )
```

```python
import jax
import jax.numpy as jnp
import numpy as np
from jax import lax
from jax.experimental import pallas as pl
from jax.experimental.pallas import tpu as pltpu
from jax.sharding import Mesh
from jax.sharding import PartitionSpec as P

AXES = ("zl", "c", "x", "y", "zh")
SIZES = (4, 2, 4, 4, 2)
NX, NY, NZ = 4, 4, 8
OWN = 88
BLK = 2 * OWN
D = 1152
M = 16 * OWN
PAIRS = 22528
F16 = jnp.float16
F32 = jnp.float32
BF16 = jnp.bfloat16


def linear(x, y, z, c):
    return int(np.ravel_multi_index((z % 4, c, x, y, z // 4), SIZES))


def pairs_of(move):
    pairs = []
    for x in range(NX):
        for y in range(NY):
            for z in range(NZ):
                for c in (0, 1):
                    to = move(x, y, z, c)
                    pairs.append((linear(x, y, z, c), linear(*to)))
    return pairs


def along_first(step):
    return pairs_of(
        lambda x, y, z, c: ((x + step) % NX, y, z, c) if c == 0 else (x, (y + step) % NY, z, c)
    )


def along_second(step):
    return pairs_of(
        lambda x, y, z, c: (x, (y + step) % NY, z, c) if c == 0 else ((x + step) % NX, y, z, c)
    )


def along_z(step):
    return pairs_of(lambda x, y, z, c: (x, y, (z + step) % NZ, c))


def other_core():
    return pairs_of(lambda x, y, z, c: (x, y, z, 1 - c))


def send(value, pairs):
    return lax.ppermute(value, AXES, pairs)


def normalize_kernel(img_ref, txt_ref, *out_refs):
    for k, ref in enumerate((img_ref, txt_ref)):
        v = ref[...]
        norm = jnp.sqrt(jnp.sum(v * v, axis=1, keepdims=True) + 1e-06)
        out_refs[k][...] = (v / norm).astype(BF16)


def normalize(images, texts):
    return pl.pallas_call(
        normalize_kernel,
        out_shape=(jax.ShapeDtypeStruct((OWN, D), BF16),) * 2,
        name="normalize",
    )(images, texts)


def project_kernel(sc_ref, lean_ref, img_ref, txt_ref, gi_ref, gt_ref, oi_ref, ot_ref):
    factor = sc_ref[0]
    lean = lean_ref[0] * 16.0
    for v_ref, g_ref, o_ref in ((img_ref, gi_ref, oi_ref), (txt_ref, gt_ref, ot_ref)):
        v = v_ref[...]
        norm = jnp.sqrt(jnp.sum(v * v, axis=1, keepdims=True) + 1e-06)
        unit = v / norm
        g = factor * (g_ref[...] + lean * unit.astype(BF16).astype(F32))
        o_ref[...] = (g - unit * jnp.sum(unit * g, axis=1, keepdims=True)) / norm


def project(scale, lean, images, texts, gi, gt):
    smem = pl.BlockSpec(memory_space=pltpu.SMEM)
    vmem = pl.BlockSpec(memory_space=pltpu.VMEM)
    out = jax.ShapeDtypeStruct((OWN, D), F32)
    return pl.pallas_call(
        project_kernel,
        out_shape=(out, out),
        in_specs=[smem, smem, vmem, vmem, vmem, vmem],
        out_specs=(vmem, vmem),
        name="project",
    )(scale, lean, images, texts, gi, gt)


LINE = (0, -1, 1, 2)
ACROSS = (0, 1, -1, 2)
TXT_AT = (0, -1, 1, 4, 2, -3, -2, 3)
BLOCKS = 16


def block_ids():
    x, y, c = (lax.axis_index(name) for name in ("x", "y", "c"))
    zl, zh = lax.axis_index("zl"), lax.axis_index("zh")
    z = zh * 4 + zl
    imgs, txts = [], []
    for b in ACROSS:
        for a in LINE:
            px = lax.rem(x + jnp.where(c == 0, a % NX, b % NX), NX)
            py = lax.rem(y + jnp.where(c == 0, b % NY, a % NY), NY)
            imgs.append((((zl * 2 + c) * NX + px) * NY + py) * 2 + zh)
    for k in (c, 1 - c):
        for dz in TXT_AT:
            pz = lax.rem(z + dz % NZ, NZ)
            txts.append(((x * NY + y) * 2 + lax.div(pz, 4)) * 8 + lax.rem(pz, 4) * 2 + k)
    return imgs, txts


ROWS = 4 * OWN
HALF = M // 2


def spread(ids, shape, dim):
    at = lax.broadcasted_iota(jnp.int32, shape, dim)
    rows = jnp.zeros(shape, jnp.int32)
    for k, block in enumerate(ids):
        rows = jnp.where(at >= k * OWN, (block - k) * OWN, rows)
    return rows + at


def load_all(parts, whole, sem):
    loads = []
    at = 0
    for k, ref in enumerate(parts):
        n = ref.shape[0]
        loads.append(pltpu.make_async_copy(ref, whole.at[pl.ds(at, n)], sem.at[k]))
        at += n
    for load in loads:
        load.start()
    return loads


def img_grad(coef, img, txt, at, lean):
    g = jnp.dot(coef[at, :], txt[...], preferred_element_type=F32)
    return g - lean * img[at, :].astype(F32)


def txt_grad(coef, img, txt, start, size, lean):
    g = lax.dot_general(
        coef[:, start : start + size], img[...], (((0,), (0,)), ((), ())), preferred_element_type=F32
    )
    return g - lean * txt[pl.ds(start, size), :].astype(F32)


def score_kernel(sc_ref, bi_ref, lean_ref, *refs):
    imgs, txts = refs[:4], refs[4:10]
    coef_ref, gw_ref, gu_ref, gd_ref = refs[10:14]
    img, txt, coef, gt, last, img_sem, txt_sem, out_sem = refs[14:]
    factor = sc_ref[0] * LOG2E
    offset = bi_ref[0] * LOG2E
    lean = lean_ref[0]
    loads = load_all(txts, txt, txt_sem) + load_all(imgs, img, img_sem)
    img_ids, txt_ids = block_ids()
    cid = spread(txt_ids, (1, M), 1)
    for load in loads:
        load.wait()
    total = jnp.zeros((8, M), F32)
    stores = []

    def keep(src, dst):
        store = pltpu.make_async_copy(src, dst, out_sem.at[len(stores)])
        store.start()
        stores.append(store)

    for k in range(M // ROWS):
        at = pl.ds(k * ROWS, ROWS)
        s = lax.dot_general(
            img[at, :], txt[...], (((1,), (1,)), ((), ())), preferred_element_type=F32
        )
        x = s * factor + offset
        e = jnp.exp2(x)
        u = 1.0 + e
        r = 1.0 / u
        label = spread(img_ids[4 * k : 4 * k + 4], (ROWS, 1), 0) == cid
        coef[at, :] = jnp.where(label, -r, e * r).astype(BF16)
        four = u.reshape(ROWS // 32, 4, 8, M)
        four = (four[:, 0] * four[:, 1]) * (four[:, 2] * four[:, 3])
        total = total + jnp.sum(jnp.log2(four), axis=0)
        total = total - jnp.sum(jnp.where(label, x, 0.0).reshape(ROWS // 8, 8, M), axis=0)
        keep(coef.at[at], coef_ref.at[at])
    part = total[:, :128]
    for k in range(1, M // 128):
        part = part + total[:, k * 128 : (k + 1) * 128]
    last[...] = jnp.zeros((8, D), F32)
    last[:, :128] = part * LN2
    keep(last, gw_ref.at[pl.ds(HALF, 8)])
    at = pl.ds(0, HALF)
    gt[at, :] = txt_grad(coef, img, txt, HALF, HALF, lean)
    keep(gt.at[at], gw_ref.at[at])
    at = pl.ds(HALF, ROWS)
    gt[at, :] = txt_grad(coef, img, txt, ROWS, ROWS, lean)
    keep(gt.at[pl.ds(HALF, BLK)], gu_ref)
    keep(gt.at[pl.ds(HALF + BLK, BLK)], gd_ref)
    for store in stores:
        store.wait()


LOG2E = 1.4426950408889634
LN2 = 0.6931471805599453
SMEM = pl.BlockSpec(memory_space=pltpu.SMEM)
VMEM = pl.BlockSpec(memory_space=pltpu.VMEM)
ANY = pl.BlockSpec(memory_space=pl.ANY)


def f32(rows):
    return jax.ShapeDtypeStruct((rows, D), F32)


def score(scale, bias, lean, imgs, txts):
    return pl.pallas_call(
        score_kernel,
        out_shape=(
            jax.ShapeDtypeStruct((M, M), BF16),
            f32(HALF + 8),
            f32(BLK),
            f32(BLK),
        ),
        in_specs=[SMEM] * 3 + [ANY] * 10,
        out_specs=(ANY,) * 4,
        scratch_shapes=[
            pltpu.VMEM((M, D), BF16),
            pltpu.VMEM((M, D), BF16),
            pltpu.VMEM((M, M), BF16),
            pltpu.VMEM((3 * ROWS, D), F32),
            pltpu.VMEM((8, D), F32),
            pltpu.SemaphoreType.DMA((4,)),
            pltpu.SemaphoreType.DMA((6,)),
            pltpu.SemaphoreType.DMA((M // ROWS + 4,)),
        ],
        compiler_params=pltpu.CompilerParams(vmem_limit_bytes=48 * 2**20),
        cost_estimate=pl.CostEstimate(
            flops=4 * M * M * D, bytes_accessed=12 * M * D, transcendentals=3 * M * M
        ),
        name="score",
    )(scale, bias, lean, *imgs, *txts)


def across_kernel(lean_ref, coef_ref, *refs):
    imgs, txts, out_refs = refs[:3], refs[3:9], refs[9:12]
    img, txt, coef, gi, img_sem, txt_sem, coef_sem, out_sem = refs[12:]
    lean = lean_ref[0]
    loads = [pltpu.make_async_copy(coef_ref.at[pl.ds(ROWS, 3 * ROWS)], coef, coef_sem)]
    loads[0].start()
    loads += load_all(txts, txt, txt_sem) + load_all(imgs, img, img_sem)
    for load in loads:
        load.wait()
    stores = []
    for k, dst in enumerate(out_refs):
        at = pl.ds(k * ROWS, ROWS)
        gi[at, :] = img_grad(coef, img, txt, at, lean)
        store = pltpu.make_async_copy(gi.at[at], dst, out_sem.at[k])
        store.start()
        stores.append(store)
    for store in stores:
        store.wait()


def across(lean, coef, imgs, txts):
    return pl.pallas_call(
        across_kernel,
        out_shape=(f32(ROWS),) * 3,
        in_specs=[SMEM] + [ANY] * 10,
        out_specs=(ANY,) * 3,
        scratch_shapes=[
            pltpu.VMEM((3 * ROWS, D), BF16),
            pltpu.VMEM((M, D), BF16),
            pltpu.VMEM((3 * ROWS, M), BF16),
            pltpu.VMEM((3 * ROWS, D), F32),
            pltpu.SemaphoreType.DMA((3,)),
            pltpu.SemaphoreType.DMA((6,)),
            pltpu.SemaphoreType.DMA,
            pltpu.SemaphoreType.DMA((3,)),
        ],
        compiler_params=pltpu.CompilerParams(vmem_limit_bytes=24 * 2**20),
        cost_estimate=pl.CostEstimate(
            flops=2 * 3 * ROWS * M * D, bytes_accessed=8 * M * D, transcendentals=0
        ),
        name="across",
    )(lean, coef, *imgs, *txts)


def near_kernel(lean_ref, coef_ref, *refs):
    imgs, txts, gl_ref, gf_ref = refs[:4], refs[4:10], refs[10], refs[11]
    img, txt, coef, gi, gt, img_sem, txt_sem, coef_sem, out_sem = refs[12:]
    lean = lean_ref[0]
    loads = [pltpu.make_async_copy(coef_ref, coef, coef_sem)]
    loads[0].start()
    loads += load_all(imgs, img, img_sem) + load_all(txts, txt, txt_sem)
    for load in loads:
        load.wait()
    gt[...] = txt_grad(coef, img, txt, 0, ROWS, lean)
    first = pltpu.make_async_copy(gt, gf_ref, out_sem.at[0])
    first.start()
    gi[...] = img_grad(coef, img, txt, pl.ds(0, ROWS), lean)
    second = pltpu.make_async_copy(gi, gl_ref, out_sem.at[1])
    second.start()
    first.wait()
    second.wait()


def nearby(lean, coef, imgs, txts):
    return pl.pallas_call(
        near_kernel,
        out_shape=(f32(ROWS),) * 2,
        in_specs=[SMEM] + [ANY] * 11,
        out_specs=(ANY,) * 2,
        scratch_shapes=[
            pltpu.VMEM((M, D), BF16),
            pltpu.VMEM((M, D), BF16),
            pltpu.VMEM((M, M), BF16),
            pltpu.VMEM((ROWS, D), F32),
            pltpu.VMEM((ROWS, D), F32),
            pltpu.SemaphoreType.DMA((4,)),
            pltpu.SemaphoreType.DMA((6,)),
            pltpu.SemaphoreType.DMA,
            pltpu.SemaphoreType.DMA((2,)),
        ],
        compiler_params=pltpu.CompilerParams(vmem_limit_bytes=24 * 2**20),
        cost_estimate=pl.CostEstimate(
            flops=M * M * D, bytes_accessed=12 * M * D, transcendentals=0
        ),
        name="nearby",
    )(lean, coef, *imgs, *txts)


def tie(*values):
    return lax.optimization_barrier(values)


def on_device(images, texts, scale, bias):
    middle = jax.nn.sigmoid(bias)
    low_end = jax.nn.sigmoid(bias - scale * np.float32(np.sqrt(3 / D)))
    high_end = jax.nn.sigmoid(bias + scale * np.float32(np.sqrt(3 / D)))
    slope = (2 / 3) * middle * (1 - middle)
    slope = slope + (1 / 6) * (low_end * (1 - low_end) + high_end * (1 - high_end))
    lean = scale * slope * np.float32(M / D)

    img, txt = normalize(images, texts)
    swap = other_core()

    t4 = send(txt, along_z(4))
    i_n, i_p = send(img, along_first(1)), send(img, along_first(-1))
    i2 = send(img, along_first(-2))
    tp = send(txt, along_z(-1))
    txt_late, i_n = tie(txt, i_n)
    tn = send(txt_late, along_z(1))
    line = jnp.concatenate([img, i_n, i_p, i2])
    qp, qn = send(line, along_second(-1)), send(line, along_second(1))
    line_late, tp = tie(line, tp)
    q2 = send(line_late, along_second(-2))
    up = send(jnp.concatenate([tp, t4]), along_z(-1))
    down = send(jnp.concatenate([tn, t4]), along_z(1))
    fan = jnp.concatenate([txt, tn, tp, t4])
    fan, qp = tie(fan, qp)
    fan_w = send(fan, swap)
    up_w, down_w = send(up, swap), send(down, swap)

    imgs = (line, qp, qn, q2)
    txts = (fan, up, down, fan_w, up_w, down_w)
    coef, gw, gup, gdown = score(scale, bias, lean, imgs, txts)

    def low16(v):
        return v.astype(F16)

    def wide(v):
        return v.astype(F32)

    def limbs(value):
        high = jnp.floor(value / 2048.0)
        rest = value - 2048.0 * high
        middle = jnp.floor(rest)
        last = jnp.floor((rest - middle) * 2048.0)
        return jnp.concatenate([high, middle, last], axis=1)

    def value_of(parts):
        return parts[:, :128] * 2048.0 + (parts[:, 128:256] + parts[:, 256:] / 2048.0)

    def tagged(rows, parts):
        return jnp.concatenate([low16(rows), low16(jnp.pad(parts, ((0, 0), (0, D - 384))))])

    def tag_of(message):
        return wide(message[-8:, :384])

    loss = gw[HALF:, :128]
    gw = send(gw, swap)
    loss = loss + gw[HALF:, :128]
    gp, gn, g2 = across(lean, coef, imgs[1:], txts)
    m_up = low16(gup + gw[ROWS : ROWS + BLK])
    m_down = low16(gdown + gw[ROWS + BLK : HALF])
    from_n = send(m_up, along_z(1))
    from_p = send(m_down, along_z(-1))
    tag = limbs(loss)
    r2 = send(tagged(g2, tag), along_second(2))
    rp = send(tagged(gp, tag), along_second(1))
    rn = send(tagged(gn, tag), along_second(-1))
    late, m_up, m_down, gn = tie(coef, m_up, m_down, gn)
    gline, gfan = nearby(lean, late, imgs, txts)
    gfan = gfan + gw[:ROWS]
    fan_4 = gfan[3 * OWN :] + wide(from_n[OWN:]) + wide(from_p[OWN:])
    fan_p = gfan[2 * OWN : 3 * OWN] + wide(from_n[:OWN])
    fan_n = gfan[OWN : 2 * OWN] + wide(from_p[:OWN])
    e4 = send(low16(fan_4), along_z(4))
    ep = send(low16(fan_p), along_z(1))
    en = send(low16(fan_n), along_z(-1))
    gline = gline + (wide(rp[:ROWS]) + wide(rn[:ROWS]) + wide(r2[:ROWS]))
    tag = limbs(value_of(tag + tag_of(rp) + tag_of(rn) + tag_of(r2)))
    d2 = send(tagged(gline[3 * OWN :], tag), along_first(2))
    dp = send(tagged(gline[2 * OWN : 3 * OWN], tag), along_first(1))
    dn = send(tagged(gline[OWN : 2 * OWN], tag), along_first(-1))
    loss = value_of(tag + tag_of(dp) + tag_of(dn) + tag_of(d2))
    loss = lax.all_to_all(jnp.tile(loss, (NZ, 1)), ("zh", "zl"), 0, 0, tiled=True)
    txt_sum = gfan[:OWN] + (wide(e4) + wide(ep) + wide(en))
    img_sum = gline[:OWN] + (wide(d2[:OWN]) + wide(dp[:OWN]) + wide(dn[:OWN]))
    image_grad, text_grad = project(scale, lean, images, texts, img_sum, txt_sum)
    loss = (jnp.sum(loss) / (PAIRS * PAIRS)).reshape(1)
    return (loss, image_grad, text_grad)


def solution(mesh):
    fine = Mesh(np.asarray(mesh.devices).reshape(SIZES), AXES)
    img = P(("zl", "c", "x", "y", "zh"), None)
    txt = P(("x", "y", "zh", "zl", "c"), None)
    return jax.shard_map(
        on_device,
        mesh=fine,
        in_specs=(img, txt, P(), P()),
        out_specs=(P(), img, txt),
        check_vma=False,
    )
```
